128 devices in a mesh: seq: 32 (over x, y, core), head: 4 (over z).
Axes of the slice: x: 4, y: 4, z: 4, core: 2. Of those that a mesh axis runs over, the one named last changes fastest.
Arguments:
- queries: bfloat16 [98304, 4096], P('seq', 'head'), may hold values from -6 to 6
- keys: bfloat16 [98304, 4096], P('seq', 'head'), may hold values from -6 to 6
- values: bfloat16 [98304, 4096], P('seq', 'head'), may hold values from -40 to 40
- gain: float32 [4096], P('head'), may hold values from 0.1 to 1.9
- placement: int32 [768], P('seq'), may hold values from 0 to 767, as said below
- segments: int32 [768], P('seq'), may hold values from 0 to 7, never falling along the last dimension, each value on 1 to 192 neighbouring positions
Outputs:
- scored: bfloat16 [98304, 4096], P('seq', 'head')
The draws below stay inside these ranges and needn't reach their ends.
Inputs may be any that keep to these rules, and one draw needn't show every extreme that they name: `placement`: together a permutation of the 768 sequence blocks; the blocks of loader d are entries d * 24 to (d + 1) * 24 - 1, those of owner o are o * 24 to (o + 1) * 24 - 1; a loader holds exactly 1 block of every owner it holds any of, and none of the others. `segments`: never falling along the sequence; every document has 1 to 192 blocks.
All inputs are finite; a program needn't handle non-finite values.
Results may differ from the reference program's by a relative error of at most 0.0049.
Values may be sent and summed in bfloat16 or wider, within the bound.
No kernel may reach another device: no remote copies, remote signals or barrier semaphores. Data moves between devices by JAX's collectives and lax.ppermute only.
A program may use at most 192 MiB of HBM per device.

```python
import math
import jax
import jax.numpy as jnp
import numpy as np
from jax import lax

HEADS = 32
HD = 128
BLOCK = 128
BLOCKS_DEV = 24
NBLOCK = 768
TOKENS = 98304
WIDTH = 4096
DOCS = 8
DOC_MOST = 192


def draw_placement(key, part):
    owner_count = NBLOCK // BLOCKS_DEV
    slot_cap = (BLOCKS_DEV + owner_count - 1) // owner_count
    group_count = BLOCKS_DEV // slot_cap
    key_one, key_two, key_three = jax.random.split(key, 3)
    shuffled = jax.random.permutation(key_one, owner_count).astype(jnp.int32)
    shift_ids = jnp.arange(owner_count, dtype=jnp.int32)
    priority = jnp.where(shift_ids == owner_count // 2, 0, jnp.where(shift_ids == 1, 1, jnp.where(shift_ids == owner_count - 1, 2, 3 + shuffled))).astype(jnp.int32)
    shift_table = jnp.argsort(priority * owner_count + shift_ids, stable=True).astype(jnp.int32)[:group_count]
    owner_keys = jax.random.split(key_two, owner_count)
    block_rank = jax.vmap(lambda owner_key: jax.random.permutation(owner_key, BLOCKS_DEV))(owner_keys)
    owner_ids = jnp.arange(owner_count, dtype=jnp.int32)[:, None]
    loader_of = (owner_ids + shift_table[block_rank // slot_cap]) % owner_count
    tie_break = jax.random.permutation(key_three, NBLOCK)
    sort_key = loader_of.reshape(-1).astype(jnp.int32) * NBLOCK + tie_break.astype(jnp.int32)
    ranking = jnp.argsort(sort_key, stable=True)
    return ranking.astype(jnp.int32)


def draw_values(key, part):
    head_ids = jnp.arange(HEADS * HD) // HD
    head_ramp = head_ids.astype(jnp.float32) / max(HEADS - 1, 1)
    base_draw = jnp.clip(jax.random.normal(key, (TOKENS, HEADS * HD), jnp.float32), -4.0, 4.0)
    return (base_draw * jnp.power(3.0, head_ramp)[None, :]).astype(jnp.bfloat16)


def block_scale(rng, shape, pieces, low, largest):
    loudness = 1.0
    for dim, parts in pieces:
        steps = jax.random.uniform(jax.random.fold_in(jax.random.fold_in(rng, 6), dim), (parts,), jnp.float32, low / len(pieces), largest / len(pieces))
        loudness = loudness * jnp.repeat(jnp.exp(steps), shape[dim] // parts).reshape((-1,) + (1,) * (len(shape) - 1 - dim))
    return loudness


def length_profile(number_of, total, reach, skew):
    portions = [(1 << 20) // math.isqrt(grade ** skew) + 1 for grade in range(2, number_of + 1)]
    surplus, counts = total - reach - (number_of - 1), [1] * (number_of - 1)
    while surplus > 0:
        free = [i for i in range(number_of - 1) if counts[i] < reach]
        whole, remaining = sum([portions[i] for i in free]), surplus
        for i in free:
            addition = min(reach - counts[i], max(1, remaining * portions[i] // whole), surplus)
            counts[i] = counts[i] + addition
            surplus = surplus - addition
    return np.array([reach] + counts)


def uneven_parts(stream_key, count, total, limit, skew):
    if count == 2:
        one = jax.random.randint(stream_key, (), max(1, total - limit), min(limit, total - 1) + 1)
        return jnp.stack([one, total - one])
    sizes = jnp.asarray(length_profile(count, total, limit, skew), jnp.int32)
    pairs = (count - 1) // 2
    donor, sink = sizes[1:1 + 2 * pairs:2], sizes[2:2 + 2 * pairs:2]
    slack = jnp.minimum(donor - 1, limit - sink)
    passed = jax.random.randint(jax.random.fold_in(stream_key, 1), (pairs,), 0, 1 << 20) % (slack + 1)
    sizes = sizes.at[1:1 + 2 * pairs:2].set(donor - passed).at[2:2 + 2 * pairs:2].set(sink + passed)
    return sizes[jax.random.permutation(jax.random.fold_in(stream_key, 2), count)]


def bell_draw(rng, dims, spread, most, cuts=(), kind=jnp.bfloat16):
    result = spread * jax.random.normal(rng, dims, jnp.float32)
    if cuts:
        result = result * block_scale(rng, dims, cuts, -0.22, 0.18)
    return jnp.clip(result, -most, most).astype(kind)


def setup_inputs(seed: int = 0) -> dict:
    arg_keys = jax.random.split(jax.random.key(seed), 7)
    return {
        "queries": bell_draw(arg_keys[0], (TOKENS, WIDTH), 1.0, 6.0, ((0, 32), (1, 4))),
        "keys": bell_draw(arg_keys[1], (TOKENS, WIDTH), 1.0, 6.0, ((0, 32), (1, 4))),
        "values": draw_values(jax.random.fold_in(arg_keys[6], 71), 0),
        "gain": jnp.clip(1.0 + 0.18 * jax.random.normal(arg_keys[3], (WIDTH,), jnp.float32), 0.1, 1.9),
        "placement": draw_placement(jax.random.fold_in(arg_keys[6], 71), 0),
        "segments": jnp.searchsorted(jnp.cumsum(uneven_parts(arg_keys[5], DOCS, NBLOCK, DOC_MOST, 0)), jnp.arange(NBLOCK), side="right").astype(jnp.int32),
    }


def rounded(matrix):
    return lax.optimization_barrier(matrix.astype(jnp.bfloat16)).astype(jnp.float32)

def reference(queries, keys, values, gain, placement, segments):
    inverse = jnp.zeros((NBLOCK,), jnp.int32).at[placement].set(jnp.arange(NBLOCK, dtype=jnp.int32))
    query_grid = queries.reshape(NBLOCK, BLOCK, HEADS, HD)
    key_grid = keys.reshape(NBLOCK, BLOCK, HEADS, HD)
    value_grid = values.reshape(NBLOCK, BLOCK, HEADS, HD)
    causal = jnp.tril(jnp.ones((BLOCK, BLOCK), dtype=bool))

    def per_head(head_index):
        query_head = jnp.take(lax.dynamic_index_in_dim(query_grid, head_index, 2, keepdims=False), inverse, axis=0).astype(jnp.float32)
        key_head = jnp.take(lax.dynamic_index_in_dim(key_grid, head_index, 2, keepdims=False), inverse, axis=0).astype(jnp.float32)
        value_head = jnp.take(lax.dynamic_index_in_dim(value_grid, head_index, 2, keepdims=False), inverse, axis=0).astype(jnp.float32)
        scores = jnp.einsum('ntd,nsd->nts', query_head, key_head)
        scores = rounded(jnp.where(causal[None], scores, jnp.zeros((), jnp.float32)))
        local = jnp.einsum('nts,nsd->ntd', scores, value_head)
        states = jnp.einsum('nsd,nse->nde', key_head, value_head)

        def advance(carry, block_item):
            running, prev_seg = carry
            state, seg = block_item
            prefix = jnp.where(seg == prev_seg, running, jnp.zeros_like(running))
            return ((prefix + state, seg), prefix)
        start = (jnp.zeros((HD, HD), jnp.float32), jnp.array(-1, dtype=jnp.int32))
        _, prefix = lax.scan(advance, start, (states, segments))
        carried = rounded(prefix)
        attended = local + jnp.einsum('ntd,nde->nte', query_head, carried)
        return jnp.take(attended, placement, axis=0)
    attended = lax.map(per_head, jnp.arange(HEADS, dtype=jnp.int32))
    square_sum = lax.optimization_barrier(jnp.sum(attended * attended, axis=(0, 3)))
    scaling = lax.rsqrt(square_sum / (HEADS * HD) + 1e-05)
    normed = attended * scaling[None, :, :, None] * gain.reshape(HEADS, 1, 1, HD)
    return jnp.moveaxis(normed, 0, 2).reshape(TOKENS, HEADS * HD).astype(jnp.bfloat16)
```

```python
import jax
import jax.numpy as jnp
from jax import lax
from jax.experimental import pallas as pl
from jax.experimental.pallas import tpu as pltpu
from jax.sharding import PartitionSpec as P

HD = 128
BLOCK = 128
BLOCKS_DEV = 24
HEADS_DEV = 8
SEQ = 32
NBLOCK = SEQ * BLOCKS_DEV
FEATURES = HEADS_DEV * HD
SLICE = FEATURES // SEQ
STEP = 3
MIB = 1 << 20
F32 = jnp.float32
BF16 = jnp.bfloat16


def params(mib):
    return pltpu.CompilerParams(vmem_limit_bytes=mib * MIB)


def head_cols(h):
    return slice(h * HD, (h + 1) * HD)


def block_rows(j):
    return slice(j * BLOCK, (j + 1) * BLOCK)


def states_kernel(k_ref, v_ref, out_ref):
    for j in range(STEP):
        for h in range(HEADS_DEV):
            state = lax.dot_general(
                k_ref[block_rows(j), head_cols(h)],
                v_ref[block_rows(j), head_cols(h)],
                (((0,), (0,)), ((), ())),
                preferred_element_type=F32,
            ).astype(BF16)
            parts = HD // SLICE
            out_ref[h * parts : (h + 1) * parts, j] = state.reshape(parts, SLICE, HD)


def states(keys, values):
    rows = pl.BlockSpec((STEP * BLOCK, FEATURES), lambda i: (i, 0))
    return pl.pallas_call(
        states_kernel,
        grid=(BLOCKS_DEV // STEP,),
        in_specs=[rows, rows],
        out_specs=pl.BlockSpec((SEQ, STEP, SLICE, HD), lambda i: (0, i, 0, 0)),
        out_shape=jax.ShapeDtypeStruct((SEQ, BLOCKS_DEV, SLICE, HD), BF16),
        compiler_params=params(58),
        cost_estimate=pl.CostEstimate(
            flops=2 * BLOCKS_DEV * HEADS_DEV * HD**3, bytes_accessed=18 * MIB, transcendentals=0
        ),
        name="block_states",
    )(keys, values)


def local_kernel(q_ref, k_ref, v_ref, out_ref):
    row = lax.broadcasted_iota(jnp.int32, (BLOCK, BLOCK), 0)
    col = lax.broadcasted_iota(jnp.int32, (BLOCK, BLOCK), 1)
    causal = col <= row
    for j in range(STEP):
        for h in range(HEADS_DEV):
            at = (block_rows(j), head_cols(h))
            scores = lax.dot_general(
                q_ref[at], k_ref[at], (((1,), (1,)), ((), ())), preferred_element_type=F32
            )
            scores = jnp.where(causal, scores, 0.0).astype(BF16)
            out_ref[at] = jnp.dot(scores, v_ref[at], preferred_element_type=F32)


def local_part(queries, keys, values):
    rows = pl.BlockSpec((STEP * BLOCK, FEATURES), lambda i: (i, 0))
    return pl.pallas_call(
        local_kernel,
        grid=(BLOCKS_DEV // STEP,),
        in_specs=[rows, rows, rows],
        out_specs=rows,
        out_shape=jax.ShapeDtypeStruct((BLOCKS_DEV * BLOCK, FEATURES), F32),
        compiler_params=params(58),
        cost_estimate=pl.CostEstimate(
            flops=4 * BLOCKS_DEV * HEADS_DEV * HD**3, bytes_accessed=30 * MIB, transcendentals=0
        ),
        name="local_part",
    )(queries, keys, values)


def prefix_kernel(plan_ref, states_ref, out_ref):
    rows = states_ref.shape[1]

    def step(g, carry):
        total, last = carry
        block = plan_ref[0, g]
        segment = plan_ref[1, g]
        total = jnp.where(segment == last, total, 0.0)
        out_ref[block] = total.astype(BF16)
        return total + states_ref[block].astype(F32), segment

    lax.fori_loop(
        0, NBLOCK, step, (jnp.zeros((rows, HD), F32), jnp.int32(-1)), unroll=4
    )


def prefix(plan, got):
    rows = 16
    part = pl.BlockSpec((NBLOCK, rows, HD), lambda i, plan: (0, i, 0))
    return pl.pallas_call(
        prefix_kernel,
        grid_spec=pltpu.PrefetchScalarGridSpec(
            num_scalar_prefetch=1, grid=(SLICE // rows,), in_specs=[part], out_specs=part
        ),
        out_shape=jax.ShapeDtypeStruct((NBLOCK, SLICE, HD), BF16),
        compiler_params=params(58),
        cost_estimate=pl.CostEstimate(
            flops=NBLOCK * SLICE * HD * 2, bytes_accessed=12 * MIB, transcendentals=0
        ),
        name="prefix",
    )(plan, got)


def cross_kernel(q_ref, local_ref, carried_ref, out_ref, square_ref):
    for j in range(STEP):
        squares = jnp.zeros((BLOCK, HD), F32)
        for h in range(HEADS_DEV):
            at = (block_rows(j), head_cols(h))
            parts = HD // SLICE
            carried = carried_ref[h * parts : (h + 1) * parts, j].reshape(HD, HD)
            attended = local_ref[at] + jnp.dot(q_ref[at], carried, preferred_element_type=F32)
            out_ref[at] = attended
            squares = squares + attended * attended
        square_ref[0, j : j + 1, :] = jnp.sum(squares.T, axis=0, keepdims=True)


def cross_part(queries, local, carried):
    rows = pl.BlockSpec((STEP * BLOCK, FEATURES), lambda i: (i, 0))
    return pl.pallas_call(
        cross_kernel,
        grid=(BLOCKS_DEV // STEP,),
        in_specs=[
            rows,
            rows,
            pl.BlockSpec((SEQ, STEP, SLICE, HD), lambda i: (0, i, 0, 0)),
        ],
        out_specs=[rows, pl.BlockSpec((1, STEP, BLOCK), lambda i: (i, 0, 0))],
        out_shape=[
            jax.ShapeDtypeStruct((BLOCKS_DEV * BLOCK, FEATURES), F32),
            jax.ShapeDtypeStruct((BLOCKS_DEV // STEP, STEP, BLOCK), F32),
        ],
        compiler_params=params(58),
        cost_estimate=pl.CostEstimate(
            flops=2 * BLOCKS_DEV * HEADS_DEV * HD**3, bytes_accessed=36 * MIB, transcendentals=0
        ),
        name="cross_part",
    )(queries, local, carried)


def finish_kernel(width, attended_ref, gain_ref, *refs):
    square_refs, out_ref = refs[:-1], refs[-1]
    total = square_refs[0][0]
    for ref in square_refs[1:]:
        total = total + ref[0]
    scaling = lax.rsqrt(total / width + 1e-05)
    for j in range(STEP):
        factor = jnp.broadcast_to(scaling[j : j + 1, :], (HD, BLOCK)).T
        for h in range(HEADS_DEV):
            at = (block_rows(j), head_cols(h))
            out_ref[at] = (attended_ref[at] * factor * gain_ref[:, head_cols(h)]).astype(BF16)


def finish(attended, gain, squares, width):
    rows = pl.BlockSpec((STEP * BLOCK, FEATURES), lambda i: (i, 0))
    sums = pl.BlockSpec((1, STEP, BLOCK), lambda i: (i, 0, 0))
    return pl.pallas_call(
        lambda *refs: finish_kernel(width, *refs),
        grid=(BLOCKS_DEV // STEP,),
        in_specs=[rows, pl.BlockSpec((1, FEATURES), lambda i: (0, 0))] + [sums] * len(squares),
        out_specs=rows,
        out_shape=jax.ShapeDtypeStruct((BLOCKS_DEV * BLOCK, FEATURES), BF16),
        compiler_params=params(58),
        name="finish_rows",
    )(attended, gain.reshape(1, FEATURES), *squares)


def sequence_plan(placement, segments):
    mine = lax.axis_index("seq")
    positions = jnp.arange(NBLOCK, dtype=jnp.int32)
    loaded = mine * BLOCKS_DEV + jnp.arange(BLOCKS_DEV, dtype=jnp.int32)
    block_at = jnp.sum(
        jnp.where(placement[:, None] == positions[None, :], loaded[:, None], 0), axis=0
    )
    segment_at = jnp.sum(
        jnp.where(loaded[:, None] == positions[None, :], segments[:, None], 0), axis=0
    )
    return lax.psum(jnp.stack([block_at, segment_at]), "seq")


def to_all(value):
    return lax.all_to_all(value, "seq", split_axis=0, concat_axis=0, tiled=True)


def on_device(queries, keys, values, gain, placement, segments):
    head_count = lax.axis_size("head")
    own = states(keys, values)
    got = to_all(own)
    plan = sequence_plan(placement, segments)
    local = local_part(queries, keys, values)
    carried = to_all(
        prefix(plan, got.reshape(NBLOCK, SLICE, HD)).reshape(SEQ, BLOCKS_DEV, SLICE, HD)
    )
    attended, square = cross_part(queries, local, carried)
    squares = [square] + [
        lax.ppermute(square, "head", [(i, (i + s) % head_count) for i in range(head_count)])
        for s in range(1, head_count)
    ]
    return finish(attended, gain, squares, head_count * FEATURES)


def solution(mesh):
    return jax.shard_map(
        on_device,
        mesh=mesh,
        in_specs=(
            P("seq", "head"),
            P("seq", "head"),
            P("seq", "head"),
            P("head"),
            P("seq"),
            P("seq"),
        ),
        out_specs=P("seq", "head"),
        check_vma=False,
    )
```

```python
import jax
import jax.numpy as jnp
from jax import lax
from jax.experimental import pallas as pl
from jax.experimental.pallas import tpu as pltpu
from jax.sharding import PartitionSpec as P

HD = 128
BLOCK = 128
BLOCKS_DEV = 24
HEADS_DEV = 8
SEQ = 32
NBLOCK = SEQ * BLOCKS_DEV
TOKENS_DEV = BLOCKS_DEV * BLOCK
FEATURES = HEADS_DEV * HD
SLICE = FEATURES // SEQ
PARTS = HD // SLICE
SENT = BLOCKS_DEV * SLICE
PLAN = 16
STEP = 4
STEPS = BLOCKS_DEV // STEP
MIB = 1 << 20
F32 = jnp.float32
BF16 = jnp.bfloat16
I32 = jnp.int32
VMEM = pl.BlockSpec(memory_space=pltpu.VMEM)
HBM = pl.BlockSpec(memory_space=pltpu.HBM)


def params(mib):
    return pltpu.CompilerParams(vmem_limit_bytes=mib * MIB)


def head_cols(h):
    return slice(h * HD, (h + 1) * HD)


def rows_at(start, size):
    return pl.ds(pl.multiple_of(start, size), size)


def in_vmem(value):
    return pltpu.with_memory_space_constraint(value, pltpu.VMEM)


def in_hbm(value):
    return pltpu.with_memory_space_constraint(value, pltpu.HBM)


def step_rows(c):
    return rows_at(c * STEP * BLOCK, STEP * BLOCK)


def states_kernel(
    k_ref, v_ref, place_ref, segment_ref, own_ref, k_held, v_held, plan, k_sem, v_sem
):
    def fetch(c, source, target, sem):
        return pltpu.make_async_copy(source.at[step_rows(c)], target.at[step_rows(c)], sem.at[c])

    for c in range(STEPS):
        fetch(c, k_ref, k_held, k_sem).start()
        fetch(c, v_ref, v_held, v_sem).start()
    place = place_ref[...]
    owner = lax.shift_right_logical(place * 2731, 16)
    plan[...] = jnp.zeros_like(plan)
    plan[0:1, 0:BLOCKS_DEV] = owner
    plan[1:2, 0:BLOCKS_DEV] = place - owner * BLOCKS_DEV
    plan[2:3, 0:BLOCKS_DEV] = segment_ref[...]
    own_ref[:, SENT : SENT + PLAN] = jnp.broadcast_to(
        plan[...].astype(F32).astype(BF16)[None], (SEQ, PLAN, HD)
    )

    def step(c, carry):
        fetch(c, k_ref, k_held, k_sem).wait()
        fetch(c, v_ref, v_held, v_sem).wait()
        for j in range(STEP):
            rows = rows_at((c * STEP + j) * BLOCK, BLOCK)
            for h in range(HEADS_DEV):
                state = lax.dot_general(
                    k_held[rows, head_cols(h)],
                    v_held[rows, head_cols(h)],
                    (((0,), (0,)), ((), ())),
                    preferred_element_type=F32,
                ).astype(BF16)
                own_ref[h * PARTS : (h + 1) * PARTS, rows_at((c * STEP + j) * SLICE, SLICE)] = (
                    state.reshape(PARTS, SLICE, HD)
                )
        return carry

    lax.fori_loop(0, STEPS, step, 0)


def states(keys, values, placement, segments):
    held = pltpu.VMEM((TOKENS_DEV, FEATURES), BF16)
    return pl.pallas_call(
        states_kernel,
        in_specs=[HBM, HBM, VMEM, VMEM],
        out_specs=VMEM,
        out_shape=pltpu.VMEM((SEQ, SENT + PLAN, HD), BF16),
        scratch_shapes=[
            held,
            held,
            pltpu.VMEM((PLAN, HD), I32),
            pltpu.SemaphoreType.DMA((STEPS,)),
            pltpu.SemaphoreType.DMA((STEPS,)),
        ],
        compiler_params=params(16),
        name="block_states",
    )(
        in_hbm(keys),
        in_hbm(values),
        placement.reshape(1, BLOCKS_DEV),
        segments.reshape(1, BLOCKS_DEV),
    )


def order_codes(got_ref):
    plan = got_ref[:, SENT : SENT + PLAN].astype(F32)
    owner, within, segment = plan[:, 0, :], plan[:, 1, :], plan[:, 2, :]
    real = lax.broadcasted_iota(I32, (SEQ, HD), 1) < BLOCKS_DEV
    owner = jnp.where(real, owner, -1.0)
    within = jnp.where(real, within, -1.0)
    owner_row = lax.broadcasted_iota(I32, (SEQ, HD), 0).astype(F32)
    within_row = lax.broadcasted_iota(I32, (HD, HD), 0).astype(F32)
    slot = lax.broadcasted_iota(I32, (1, HD), 1).astype(F32)
    picks, spots = [], []
    for d in range(SEQ):
        picks.append(jnp.where(owner[d : d + 1] == owner_row, 1.0, 0.0).astype(BF16))
        here = within[d : d + 1] == within_row[:SEQ]
        spots.append(
            jnp.concatenate(
                [
                    jnp.where(here, float(d), 0.0),
                    jnp.where(here, jnp.broadcast_to(slot, (SEQ, HD)), 0.0),
                    jnp.zeros((HD - 2 * SEQ, HD), F32),
                ],
                axis=0,
            ).astype(BF16)
        )
    table = lax.dot_general(
        jnp.concatenate(picks, axis=1),
        jnp.concatenate(spots, axis=1),
        (((1,), (1,)), ((), ())),
        preferred_element_type=F32,
    )
    loader = table
    slot = jnp.concatenate([table[:, SEQ:], table[:, :SEQ]], axis=1)
    return (
        loader.astype(I32),
        slot.astype(I32),
        segment.astype(I32),
    )


def prefix_kernel(got_ref, out_ref, codes, table, code_sem):
    loader, slot, segment = order_codes(got_ref)
    codes[...] = loader * 32 + slot + segment * 1024
    code_copy = pltpu.make_async_copy(codes, table, code_sem)
    code_copy.start()
    code_copy.wait()

    def owner_step(o, carry):
        total, last = carry
        for w in range(BLOCKS_DEV):
            code = table[o, w]
            loader = lax.shift_right_logical(code, 5) & 31
            slot = code & 31
            segment = lax.shift_right_logical(code, 10)
            at = (loader, rows_at(slot * SLICE, SLICE))
            total = jnp.where(segment == last, total, 0.0)
            out_ref[at] = total.astype(BF16)
            total = total + got_ref[at].astype(F32)
            last = segment
        return total, last

    lax.fori_loop(0, SEQ, owner_step, (jnp.zeros((SLICE, HD), F32), I32(-1)))


def prefix(got):
    return pl.pallas_call(
        prefix_kernel,
        in_specs=[VMEM],
        out_specs=VMEM,
        out_shape=pltpu.VMEM((SEQ, SENT, HD), BF16),
        scratch_shapes=[
            pltpu.VMEM((SEQ, HD), I32),
            pltpu.SMEM((SEQ, HD), I32),
            pltpu.SemaphoreType.DMA,
        ],
        compiler_params=params(8),
        name="prefix",
    )(in_vmem(got))


def attend_kernel(q_ref, k_ref, v_ref, carried_ref, out_ref, square_ref):
    row = lax.broadcasted_iota(I32, (BLOCK, BLOCK), 0)
    col = lax.broadcasted_iota(I32, (BLOCK, BLOCK), 1)
    causal = col <= row

    def step(c, carry):
        for j in range(STEP):
            block = c * STEP + j
            rows = rows_at(block * BLOCK, BLOCK)
            scores = [
                jnp.where(
                    causal,
                    lax.dot_general(
                        q_ref[rows, head_cols(h)],
                        k_ref[rows, head_cols(h)],
                        (((1,), (1,)), ((), ())),
                        preferred_element_type=F32,
                    ),
                    0.0,
                ).astype(BF16)
                for h in range(HEADS_DEV)
            ]
            squares = jnp.zeros((BLOCK, HD), F32)
            for h in range(HEADS_DEV):
                carried = carried_ref[
                    h * PARTS : (h + 1) * PARTS, rows_at(block * SLICE, SLICE)
                ].reshape(HD, HD)
                attended = jnp.dot(
                    jnp.concatenate([scores[h], q_ref[rows, head_cols(h)]], axis=1),
                    jnp.concatenate([v_ref[rows, head_cols(h)], carried], axis=0),
                    preferred_element_type=F32,
                )
                out_ref[rows, head_cols(h)] = attended
                squares = squares + attended * attended
            square_ref[pl.ds(block, 1), :] = jnp.sum(squares.T, axis=0, keepdims=True)
        return carry

    lax.fori_loop(0, STEPS, step, 0)


def attend(queries, keys, values, carried):
    return pl.pallas_call(
        attend_kernel,
        in_specs=[VMEM] * 4,
        out_specs=[VMEM, VMEM],
        out_shape=[
            pltpu.VMEM((TOKENS_DEV, FEATURES), F32),
            jax.ShapeDtypeStruct((BLOCKS_DEV, BLOCK), F32),
        ],
        compiler_params=params(8),
        name="attend",
    )(in_vmem(queries), in_vmem(keys), in_vmem(values), in_vmem(carried))


def finish_kernel(width, attended_ref, gain_ref, *refs):
    square_refs, (out_ref, staged, out_sem) = refs[:-3], refs[-3:]
    total = square_refs[0][...]
    for ref in square_refs[1:]:
        total = total + ref[...]
    scaling = lax.rsqrt(total / width + 1e-05)

    def give(c):
        rows = slice(c * STEP * BLOCK, (c + 1) * STEP * BLOCK)
        return pltpu.make_async_copy(staged.at[rows], out_ref.at[rows], out_sem.at[c])

    for c in range(STEPS):
        for block in range(c * STEP, (c + 1) * STEP):
            rows = slice(block * BLOCK, (block + 1) * BLOCK)
            factor = jnp.broadcast_to(scaling[block : block + 1, :], (HD, BLOCK)).T
            for h in range(HEADS_DEV):
                at = (rows, head_cols(h))
                staged[at] = (attended_ref[at] * factor * gain_ref[:, head_cols(h)]).astype(BF16)
        give(c).start()
    for c in range(STEPS):
        give(c).wait()


def finish(attended, gain, squares, width):
    return pl.pallas_call(
        lambda *refs: finish_kernel(width, *refs),
        in_specs=[VMEM] * (2 + len(squares)),
        out_specs=HBM,
        out_shape=jax.ShapeDtypeStruct((TOKENS_DEV, FEATURES), BF16),
        scratch_shapes=[
            pltpu.VMEM((TOKENS_DEV, FEATURES), BF16),
            pltpu.SemaphoreType.DMA((STEPS,)),
        ],
        compiler_params=params(12),
        name="finish_rows",
    )(in_vmem(attended), gain.reshape(1, FEATURES), *squares)


def to_all(value):
    return lax.all_to_all(value, "seq", split_axis=0, concat_axis=0, tiled=True)


def on_device(queries, keys, values, gain, placement, segments):
    head_count = lax.axis_size("head")
    got = to_all(states(keys, values, placement, segments))
    attended, square = attend(queries, keys, values, to_all(prefix(got)))
    squares = [square] + [
        lax.ppermute(square, "head", [(i, (i + s) % head_count) for i in range(head_count)])
        for s in range(1, head_count)
    ]
    return finish(attended, gain, squares, head_count * FEATURES)


def solution(mesh):
    return jax.shard_map(
        on_device,
        mesh=mesh,
        in_specs=(
            P("seq", "head"),
            P("seq", "head"),
            P("seq", "head"),
            P("head"),
            P("seq"),
            P("seq"),
        ),
        out_specs=P("seq", "head"),
        check_vma=False,
    )
```

```python
import jax
import jax.numpy as jnp
from jax import lax
from jax.experimental import pallas as pl
from jax.experimental.pallas import tpu as pltpu
from jax.sharding import PartitionSpec as P

HD = 128
BLOCK = 128
BLOCKS_DEV = 24
HEADS_DEV = 8
SEQ = 32
NBLOCK = SEQ * BLOCKS_DEV
TOKENS_DEV = BLOCKS_DEV * BLOCK
FEATURES = HEADS_DEV * HD
SLICE = FEATURES // SEQ
PARTS = HD // SLICE
SENT = BLOCKS_DEV * SLICE
PLAN = 8
STEP = 3
STEPS = BLOCKS_DEV // STEP
ATTEND_STEP = 24
GROUP = 24
OUT_AT = SEQ
SEGMENT_AT = 2 * SEQ
MIB = 1 << 20
F32 = jnp.float32
BF16 = jnp.bfloat16
I32 = jnp.int32
VMEM = pl.BlockSpec(memory_space=pltpu.VMEM)
HBM = pl.BlockSpec(memory_space=pltpu.HBM)


def params(mib):
    return pltpu.CompilerParams(vmem_limit_bytes=mib * MIB)


def head_cols(h):
    return slice(h * HD, (h + 1) * HD)


def rows_at(start, size):
    return pl.ds(pl.multiple_of(start, size), size)


def in_vmem(value):
    return pltpu.with_memory_space_constraint(value, pltpu.VMEM)


def in_hbm(value):
    return pltpu.with_memory_space_constraint(value, pltpu.HBM)


def step_rows(c):
    return rows_at(c * STEP * BLOCK, STEP * BLOCK)


def states_kernel(
    k_ref, v_ref, place_ref, segment_ref, own_ref, k_held, v_held, given, plan, k_sem, v_sem, sem
):
    def fetch(c, source, target, sem):
        return pltpu.make_async_copy(source.at[step_rows(c)], target.at[step_rows(c)], sem.at[c])

    place_copy = pltpu.make_async_copy(place_ref, given.at[0], sem.at[0])
    segment_copy = pltpu.make_async_copy(segment_ref, given.at[1], sem.at[1])
    place_copy.start()
    segment_copy.start()
    for c in range(STEPS):
        fetch(c, k_ref, k_held, k_sem).start()
        fetch(c, v_ref, v_held, v_sem).start()

    def step(c, carry):
        fetch(c, k_ref, k_held, k_sem).wait()
        fetch(c, v_ref, v_held, v_sem).wait()
        for j in range(STEP):
            rows = rows_at((c * STEP + j) * BLOCK, BLOCK)
            for h in range(HEADS_DEV):
                state = lax.dot_general(
                    k_held[rows, head_cols(h)],
                    v_held[rows, head_cols(h)],
                    (((0,), (0,)), ((), ())),
                    preferred_element_type=F32,
                ).astype(BF16)
                own_ref[h * PARTS : (h + 1) * PARTS, rows_at((c * STEP + j) * SLICE, SLICE)] = (
                    state.reshape(PARTS, SLICE, HD)
                )
        return carry

    lax.fori_loop(0, STEPS, step, 0)
    place_copy.wait()
    segment_copy.wait()
    place = given[0]
    owner = lax.shift_right_logical(place * 2731, 16)
    plan[...] = jnp.zeros_like(plan)
    plan[0:1, 0:BLOCKS_DEV] = owner
    plan[1:2, 0:BLOCKS_DEV] = place - owner * BLOCKS_DEV
    plan[2:3, SEGMENT_AT : SEGMENT_AT + BLOCKS_DEV] = given[1]
    own_ref[:, SENT : SENT + PLAN] = jnp.broadcast_to(
        plan[...].astype(F32).astype(BF16)[None], (SEQ, PLAN, HD)
    )


def states(keys, values, placement, segments):
    held = pltpu.VMEM((TOKENS_DEV, FEATURES), BF16)
    return pl.pallas_call(
        states_kernel,
        in_specs=[HBM] * 4,
        out_specs=VMEM,
        out_shape=pltpu.VMEM((SEQ, SENT + PLAN, HD), BF16),
        scratch_shapes=[
            held,
            held,
            pltpu.VMEM((2, 1, BLOCKS_DEV), I32),
            pltpu.VMEM((PLAN, HD), I32),
            pltpu.SemaphoreType.DMA((STEPS,)),
            pltpu.SemaphoreType.DMA((STEPS,)),
            pltpu.SemaphoreType.DMA((2,)),
        ],
        compiler_params=params(16),
        name="block_states",
    )(
        in_hbm(keys),
        in_hbm(values),
        in_hbm(placement.reshape(1, BLOCKS_DEV)),
        in_hbm(segments.reshape(1, BLOCKS_DEV)),
    )


def block_order(got_ref):
    plan = got_ref[:, SENT : SENT + PLAN].astype(F32)
    spot_row = lax.broadcasted_iota(I32, (SEQ, HD), 0).astype(F32)
    lane = lax.broadcasted_iota(I32, (SEQ, HD), 1)
    slot = lane.astype(F32)
    real = lane < BLOCKS_DEV
    owner_row = jnp.where(real, spot_row, -1.0)
    picks, spots = [], []
    for d in range(SEQ):
        picks.append(jnp.where(plan[d, 0:1] == owner_row, 1.0, 0.0).astype(BF16))
        here = plan[d, 1:2] == spot_row
        spots.append(
            jnp.concatenate(
                [jnp.where(here, float(d), 0.0), jnp.where(here, slot, 0.0)], axis=0
            ).astype(BF16)
        )
    found = lax.dot_general(
        jnp.concatenate(picks, axis=1),
        jnp.concatenate(spots, axis=1),
        (((1,), (1,)), ((), ())),
        preferred_element_type=F32,
    ).astype(I32)
    loader, slot = found[:, :SEQ], found[:, SEQ:]
    got_at = loader * (SENT + PLAN) + slot * SLICE
    out_at = loader * SENT + slot * SLICE
    rows = jnp.concatenate([got_at, out_at, jnp.zeros((SEQ, HD - 2 * SEQ), I32)], axis=1)
    return jnp.where(lane < SEGMENT_AT, rows, plan[:, 2, :].astype(I32))


def prefix_kernel(got_ref, out_ref, order, table, order_sem):
    order[...] = block_order(got_ref)
    order_copy = pltpu.make_async_copy(order, table, order_sem)
    order_copy.start()
    order_copy.wait()
    got_rows = got_ref.reshape(SEQ * (SENT + PLAN), HD)
    out_rows = out_ref.reshape(SEQ * SENT, HD)

    def owner_step(o, carry):
        for first in range(0, BLOCKS_DEV, GROUP):
            group = range(first, first + GROUP)

            def run(total, last, check):
                loaded = [got_rows[rows_at(table[o, w], SLICE), :] for w in group]
                before = []
                for w, state in zip(group, loaded):
                    if check:
                        segment = table[o, SEGMENT_AT + w]
                        total = jnp.where(segment == last, total, 0.0)
                        last = segment
                    before.append(total.astype(BF16))
                    total = total + state.astype(F32)
                for w, value in zip(group, before):
                    out_rows[rows_at(table[o, OUT_AT + w], SLICE), :] = value
                return total, last

            total, last = carry
            carry = lax.cond(
                table[o, SEGMENT_AT + group[-1]] == last,
                lambda total, last: run(total, last, False),
                lambda total, last: run(total, last, True),
                total,
                last,
            )
        return carry

    lax.fori_loop(0, SEQ, owner_step, (jnp.zeros((SLICE, HD), F32), I32(-1)))


def prefix(got):
    return pl.pallas_call(
        prefix_kernel,
        in_specs=[VMEM],
        out_specs=VMEM,
        out_shape=pltpu.VMEM((SEQ, SENT, HD), BF16),
        scratch_shapes=[
            pltpu.VMEM((SEQ, HD), I32),
            pltpu.SMEM((SEQ, HD), I32),
            pltpu.SemaphoreType.DMA,
        ],
        compiler_params=params(8),
        name="prefix",
    )(in_vmem(got))


def attend_kernel(q_ref, k_ref, v_ref, carried_ref, out_ref, square_ref):
    row = lax.broadcasted_iota(I32, (BLOCK, BLOCK), 0)
    col = lax.broadcasted_iota(I32, (BLOCK, BLOCK), 1)
    causal = col <= row

    def step(c, carry):
        for j in range(ATTEND_STEP):
            block = c * ATTEND_STEP + j
            rows = rows_at(block * BLOCK, BLOCK)
            scores = [
                jnp.where(
                    causal,
                    lax.dot_general(
                        q_ref[rows, head_cols(h)],
                        k_ref[rows, head_cols(h)],
                        (((1,), (1,)), ((), ())),
                        preferred_element_type=F32,
                    ),
                    0.0,
                ).astype(BF16)
                for h in range(HEADS_DEV)
            ]
            squares = jnp.zeros((BLOCK, HD), F32)
            for h in range(HEADS_DEV):
                carried = carried_ref[
                    h * PARTS : (h + 1) * PARTS, rows_at(block * SLICE, SLICE)
                ].reshape(HD, HD)
                attended = jnp.dot(
                    jnp.concatenate([scores[h], q_ref[rows, head_cols(h)]], axis=1),
                    jnp.concatenate([v_ref[rows, head_cols(h)], carried], axis=0),
                    preferred_element_type=F32,
                )
                out_ref[rows, head_cols(h)] = attended
                squares = squares + attended * attended
            square_ref[pl.ds(block, 1), :] = jnp.sum(squares.T, axis=0, keepdims=True)
        return carry

    lax.fori_loop(0, BLOCKS_DEV // ATTEND_STEP, step, 0)


def attend(queries, keys, values, carried):
    return pl.pallas_call(
        attend_kernel,
        in_specs=[VMEM] * 4,
        out_specs=[VMEM, VMEM],
        out_shape=[
            pltpu.VMEM((TOKENS_DEV, FEATURES), F32),
            jax.ShapeDtypeStruct((BLOCKS_DEV, BLOCK), F32),
        ],
        compiler_params=params(8),
        name="attend",
    )(in_vmem(queries), in_vmem(keys), in_vmem(values), in_vmem(carried))


def finish_kernel(width, attended_ref, gain_ref, *refs):
    square_refs, (out_ref, staged, out_sem) = refs[:-3], refs[-3:]
    total = square_refs[0][...]
    for ref in square_refs[1:]:
        total = total + ref[...]
    scaling = lax.rsqrt(total / width + 1e-05)

    def give(c):
        rows = slice(c * STEP * BLOCK, (c + 1) * STEP * BLOCK)
        return pltpu.make_async_copy(staged.at[rows], out_ref.at[rows], out_sem.at[c])

    for c in range(STEPS):
        for block in range(c * STEP, (c + 1) * STEP):
            rows = slice(block * BLOCK, (block + 1) * BLOCK)
            factor = jnp.broadcast_to(scaling[block : block + 1, :], (HD, BLOCK)).T
            for h in range(HEADS_DEV):
                at = (rows, head_cols(h))
                staged[at] = (attended_ref[at] * factor * gain_ref[:, head_cols(h)]).astype(BF16)
        give(c).start()
    for c in range(STEPS):
        give(c).wait()


def finish(attended, gain, squares, width):
    return pl.pallas_call(
        lambda *refs: finish_kernel(width, *refs),
        in_specs=[VMEM] * (2 + len(squares)),
        out_specs=HBM,
        out_shape=jax.ShapeDtypeStruct((TOKENS_DEV, FEATURES), BF16),
        scratch_shapes=[
            pltpu.VMEM((TOKENS_DEV, FEATURES), BF16),
            pltpu.SemaphoreType.DMA((STEPS,)),
        ],
        compiler_params=params(12),
        name="finish_rows",
    )(in_vmem(attended), gain.reshape(1, FEATURES), *squares)


def to_all(value):
    return lax.all_to_all(value, "seq", split_axis=0, concat_axis=0, tiled=True)


def on_device(queries, keys, values, gain, placement, segments):
    head_count = lax.axis_size("head")
    got = to_all(states(keys, values, placement, segments))
    attended, square = attend(queries, keys, values, to_all(prefix(got)))
    squares = [square] + [
        lax.ppermute(square, "head", [(i, (i + s) % head_count) for i in range(head_count)])
        for s in range(1, head_count)
    ]
    return finish(attended, gain, squares, head_count * FEATURES)


def solution(mesh):
    return jax.shard_map(
        on_device,
        mesh=mesh,
        in_specs=(
            P("seq", "head"),
            P("seq", "head"),
            P("seq", "head"),
            P("head"),
            P("seq"),
            P("seq"),
        ),
        out_specs=P("seq", "head"),
        check_vma=False,
    )
```

```python
import jax
import jax.numpy as jnp
from jax import lax
from jax.experimental import pallas as pl
from jax.experimental.pallas import tpu as pltpu
from jax.sharding import PartitionSpec as P

HD = 128
BLOCK = 128
BLOCKS_DEV = 24
HEADS_DEV = 8
SEQ = 32
NBLOCK = SEQ * BLOCKS_DEV
TOKENS_DEV = BLOCKS_DEV * BLOCK
FEATURES = HEADS_DEV * HD
SLICE = FEATURES // SEQ
PARTS = HD // SLICE
SENT = BLOCKS_DEV * SLICE
PLAN = 8
STEP = 3
STEPS = BLOCKS_DEV // STEP
ATTEND_STEP = 24
GROUP = 24
OUT_AT = SEQ
SEGMENT_AT = 2 * SEQ
MIB = 1 << 20
F32 = jnp.float32
BF16 = jnp.bfloat16
I32 = jnp.int32
VMEM = pl.BlockSpec(memory_space=pltpu.VMEM)
HBM = pl.BlockSpec(memory_space=pltpu.HBM)


def params(mib):
    return pltpu.CompilerParams(vmem_limit_bytes=mib * MIB)


def head_cols(h):
    return slice(h * HD, (h + 1) * HD)


def rows_at(start, size):
    return pl.ds(pl.multiple_of(start, size), size)


def in_vmem(value):
    return pltpu.with_memory_space_constraint(value, pltpu.VMEM)


def in_hbm(value):
    return pltpu.with_memory_space_constraint(value, pltpu.HBM)


def step_rows(c):
    return rows_at(c * STEP * BLOCK, STEP * BLOCK)


def states_kernel(
    q_ref, k_ref, v_ref, place_ref, segment_ref, own_ref, scores_ref, q_held, k_held, v_held, given,
    plan, q_sem, k_sem, v_sem, sem
):
    def fetch(c, source, target, sem):
        return pltpu.make_async_copy(source.at[step_rows(c)], target.at[step_rows(c)], sem.at[c])

    row = lax.broadcasted_iota(I32, (BLOCK, BLOCK), 0)
    col = lax.broadcasted_iota(I32, (BLOCK, BLOCK), 1)
    causal = col <= row
    place_copy = pltpu.make_async_copy(place_ref, given.at[0], sem.at[0])
    segment_copy = pltpu.make_async_copy(segment_ref, given.at[1], sem.at[1])
    place_copy.start()
    segment_copy.start()
    for c in range(STEPS):
        fetch(c, k_ref, k_held, k_sem).start()
        fetch(c, v_ref, v_held, v_sem).start()
        fetch(c, q_ref, q_held, q_sem).start()

    def step(c, carry):
        fetch(c, k_ref, k_held, k_sem).wait()
        fetch(c, v_ref, v_held, v_sem).wait()
        fetch(c, q_ref, q_held, q_sem).wait()
        for j in range(STEP):
            block = c * STEP + j
            rows = rows_at(block * BLOCK, BLOCK)
            for h in range(HEADS_DEV):
                turned = k_held[rows, head_cols(h)].T
                state = jnp.dot(turned, v_held[rows, head_cols(h)], preferred_element_type=F32)
                own_ref[h * PARTS : (h + 1) * PARTS, rows_at(block * SLICE, SLICE)] = (
                    state.astype(BF16).reshape(PARTS, SLICE, HD)
                )
                scores = jnp.dot(q_held[rows, head_cols(h)], turned, preferred_element_type=F32)
                scores_ref[rows, head_cols(h)] = jnp.where(causal, scores, 0.0).astype(BF16)
        return carry

    lax.fori_loop(0, STEPS, step, 0)
    place_copy.wait()
    segment_copy.wait()
    place = given[0]
    owner = lax.shift_right_logical(place * 2731, 16)
    plan[...] = jnp.zeros_like(plan)
    plan[0:1, 0:BLOCKS_DEV] = owner
    plan[1:2, 0:BLOCKS_DEV] = place - owner * BLOCKS_DEV
    plan[2:3, SEGMENT_AT : SEGMENT_AT + BLOCKS_DEV] = given[1]
    own_ref[:, SENT : SENT + PLAN] = jnp.broadcast_to(
        plan[...].astype(F32).astype(BF16)[None], (SEQ, PLAN, HD)
    )


def states(queries, keys, values, placement, segments):
    held = pltpu.VMEM((TOKENS_DEV, FEATURES), BF16)
    return pl.pallas_call(
        states_kernel,
        in_specs=[HBM] * 5,
        out_specs=[VMEM, VMEM],
        out_shape=[pltpu.VMEM((SEQ, SENT + PLAN, HD), BF16), held],
        scratch_shapes=[
            held,
            held,
            held,
            pltpu.VMEM((2, 1, BLOCKS_DEV), I32),
            pltpu.VMEM((PLAN, HD), I32),
            pltpu.SemaphoreType.DMA((STEPS,)),
            pltpu.SemaphoreType.DMA((STEPS,)),
            pltpu.SemaphoreType.DMA((STEPS,)),
            pltpu.SemaphoreType.DMA((2,)),
        ],
        compiler_params=params(22),
        name="block_states",
    )(
        in_hbm(queries),
        in_hbm(keys),
        in_hbm(values),
        in_hbm(placement.reshape(1, BLOCKS_DEV)),
        in_hbm(segments.reshape(1, BLOCKS_DEV)),
    )


def block_order(got_ref):
    plan = got_ref[:, SENT : SENT + PLAN].astype(F32)
    spot_row = lax.broadcasted_iota(I32, (SEQ, HD), 0).astype(F32)
    lane = lax.broadcasted_iota(I32, (SEQ, HD), 1)
    slot = lane.astype(F32)
    real = lane < BLOCKS_DEV
    owner_row = jnp.where(real, spot_row, -1.0)
    picks, spots = [], []
    for d in range(SEQ):
        picks.append(jnp.where(plan[d, 0:1] == owner_row, 1.0, 0.0).astype(BF16))
        here = plan[d, 1:2] == spot_row
        spots.append(
            jnp.concatenate(
                [jnp.where(here, float(d), 0.0), jnp.where(here, slot, 0.0)], axis=0
            ).astype(BF16)
        )
    found = lax.dot_general(
        jnp.concatenate(picks, axis=1),
        jnp.concatenate(spots, axis=1),
        (((1,), (1,)), ((), ())),
        preferred_element_type=F32,
    ).astype(I32)
    loader, slot = found[:, :SEQ], found[:, SEQ:]
    got_at = loader * (SENT + PLAN) + slot * SLICE
    out_at = loader * SENT + slot * SLICE
    rows = jnp.concatenate([got_at, out_at, jnp.zeros((SEQ, HD - 2 * SEQ), I32)], axis=1)
    return jnp.where(lane < SEGMENT_AT, rows, plan[:, 2, :].astype(I32))


def prefix_kernel(got_ref, out_ref, order, table, order_sem):
    order[...] = block_order(got_ref)
    order_copy = pltpu.make_async_copy(order, table, order_sem)
    order_copy.start()
    order_copy.wait()
    got_rows = got_ref.reshape(SEQ * (SENT + PLAN), HD)
    out_rows = out_ref.reshape(SEQ * SENT, HD)

    def owner_step(o, carry):
        for first in range(0, BLOCKS_DEV, GROUP):
            group = range(first, first + GROUP)

            def run(total, last, check):
                loaded = [got_rows[rows_at(table[o, w], SLICE), :] for w in group]
                before = []
                for w, state in zip(group, loaded):
                    if check:
                        segment = table[o, SEGMENT_AT + w]
                        total = jnp.where(segment == last, total, 0.0)
                        last = segment
                    before.append(total.astype(BF16))
                    total = total + state.astype(F32)
                for w, value in zip(group, before):
                    out_rows[rows_at(table[o, OUT_AT + w], SLICE), :] = value
                return total, last

            total, last = carry
            carry = lax.cond(
                table[o, SEGMENT_AT + group[-1]] == last,
                lambda total, last: run(total, last, False),
                lambda total, last: run(total, last, True),
                total,
                last,
            )
        return carry

    lax.fori_loop(0, SEQ, owner_step, (jnp.zeros((SLICE, HD), F32), I32(-1)))


def prefix(got):
    return pl.pallas_call(
        prefix_kernel,
        in_specs=[VMEM],
        out_specs=VMEM,
        out_shape=pltpu.VMEM((SEQ, SENT, HD), BF16),
        scratch_shapes=[
            pltpu.VMEM((SEQ, HD), I32),
            pltpu.SMEM((SEQ, HD), I32),
            pltpu.SemaphoreType.DMA,
        ],
        compiler_params=params(8),
        name="prefix",
    )(in_vmem(got))


def attend_kernel(q_ref, scores_ref, v_ref, carried_ref, out_ref, square_ref):
    def step(c, carry):
        for j in range(ATTEND_STEP):
            block = c * ATTEND_STEP + j
            rows = rows_at(block * BLOCK, BLOCK)
            squares = jnp.zeros((BLOCK, HD), F32)
            for h in range(HEADS_DEV):
                carried = carried_ref[
                    h * PARTS : (h + 1) * PARTS, rows_at(block * SLICE, SLICE)
                ].reshape(HD, HD)
                attended = jnp.dot(
                    jnp.concatenate(
                        [scores_ref[rows, head_cols(h)], q_ref[rows, head_cols(h)]], axis=1
                    ),
                    jnp.concatenate([v_ref[rows, head_cols(h)], carried], axis=0),
                    preferred_element_type=F32,
                )
                out_ref[rows, head_cols(h)] = attended
                squares = squares + attended * attended
            square_ref[pl.ds(block, 1), :] = jnp.sum(squares.T, axis=0, keepdims=True)
        return carry

    lax.fori_loop(0, BLOCKS_DEV // ATTEND_STEP, step, 0)


def attend(queries, scores, values, carried):
    return pl.pallas_call(
        attend_kernel,
        in_specs=[VMEM] * 4,
        out_specs=[VMEM, VMEM],
        out_shape=[
            pltpu.VMEM((TOKENS_DEV, FEATURES), F32),
            jax.ShapeDtypeStruct((BLOCKS_DEV, BLOCK), F32),
        ],
        compiler_params=params(8),
        name="attend",
    )(in_vmem(queries), in_vmem(scores), in_vmem(values), in_vmem(carried))


def finish_kernel(width, attended_ref, gain_ref, *refs):
    square_refs, (out_ref, staged, out_sem) = refs[:-3], refs[-3:]
    total = square_refs[0][...]
    for ref in square_refs[1:]:
        total = total + ref[...]
    scaling = lax.rsqrt(total / width + 1e-05)

    def give(c):
        rows = slice(c * STEP * BLOCK, (c + 1) * STEP * BLOCK)
        return pltpu.make_async_copy(staged.at[rows], out_ref.at[rows], out_sem.at[c])

    for c in range(STEPS):
        for block in range(c * STEP, (c + 1) * STEP):
            rows = slice(block * BLOCK, (block + 1) * BLOCK)
            factor = jnp.broadcast_to(scaling[block : block + 1, :], (HD, BLOCK)).T
            for h in range(HEADS_DEV):
                at = (rows, head_cols(h))
                staged[at] = (attended_ref[at] * factor * gain_ref[:, head_cols(h)]).astype(BF16)
        give(c).start()
    for c in range(STEPS):
        give(c).wait()


def finish(attended, gain, squares, width):
    return pl.pallas_call(
        lambda *refs: finish_kernel(width, *refs),
        in_specs=[VMEM] * (2 + len(squares)),
        out_specs=HBM,
        out_shape=jax.ShapeDtypeStruct((TOKENS_DEV, FEATURES), BF16),
        scratch_shapes=[
            pltpu.VMEM((TOKENS_DEV, FEATURES), BF16),
            pltpu.SemaphoreType.DMA((STEPS,)),
        ],
        compiler_params=params(12),
        name="finish_rows",
    )(in_vmem(attended), gain.reshape(1, FEATURES), *squares)


def to_all(value):
    return lax.all_to_all(value, "seq", split_axis=0, concat_axis=0, tiled=True)


def on_device(queries, keys, values, gain, placement, segments):
    head_count = lax.axis_size("head")
    own, scores = states(queries, keys, values, placement, segments)
    attended, square = attend(queries, scores, values, to_all(prefix(to_all(own))))
    squares = [square] + [
        lax.ppermute(square, "head", [(i, (i + s) % head_count) for i in range(head_count)])
        for s in range(1, head_count)
    ]
    return finish(attended, gain, squares, head_count * FEATURES)


def solution(mesh):
    return jax.shard_map(
        on_device,
        mesh=mesh,
        in_specs=(
            P("seq", "head"),
            P("seq", "head"),
            P("seq", "head"),
            P("head"),
            P("seq"),
            P("seq"),
        ),
        out_specs=P("seq", "head"),
        check_vma=False,
    )
```

```python
import jax
import jax.numpy as jnp
from jax import lax
from jax.experimental import pallas as pl
from jax.experimental.pallas import tpu as pltpu
from jax.sharding import PartitionSpec as P

HD = 128
BLOCK = 128
BLOCKS_DEV = 24
HEADS_DEV = 8
SEQ = 32
NBLOCK = SEQ * BLOCKS_DEV
TOKENS_DEV = BLOCKS_DEV * BLOCK
FEATURES = HEADS_DEV * HD
SLICE = FEATURES // SEQ
PARTS = HD // SLICE
SENT = BLOCKS_DEV * SLICE
PLAN = 16
STEP = 3
STEPS = BLOCKS_DEV // STEP
ATTEND_STEP = 24
GROUP = 24
LOADED = 8
OUT_AT = SEQ
SEGMENT_AT = 2 * SEQ
MIB = 1 << 20
F32 = jnp.float32
BF16 = jnp.bfloat16
I32 = jnp.int32
VMEM = pl.BlockSpec(memory_space=pltpu.VMEM)
HBM = pl.BlockSpec(memory_space=pltpu.HBM)


def params(mib):
    return pltpu.CompilerParams(vmem_limit_bytes=mib * MIB)


def head_cols(h):
    return slice(h * HD, (h + 1) * HD)


def rows_at(start, size):
    return pl.ds(pl.multiple_of(start, size), size)


def in_vmem(value):
    return pltpu.with_memory_space_constraint(value, pltpu.VMEM)


def in_hbm(value):
    return pltpu.with_memory_space_constraint(value, pltpu.HBM)


def step_rows(c):
    return rows_at(c * STEP * BLOCK, STEP * BLOCK)


def states_kernel(
    q_ref, k_ref, v_ref, place_ref, segment_ref, own_ref, scores_ref, q_held, k_held, v_held, given,
    plan, q_sem, k_sem, v_sem, sem
):
    def fetch(c, source, target, sem):
        return pltpu.make_async_copy(source.at[step_rows(c)], target.at[step_rows(c)], sem.at[c])

    row = lax.broadcasted_iota(I32, (BLOCK, BLOCK), 0)
    col = lax.broadcasted_iota(I32, (BLOCK, BLOCK), 1)
    causal = col <= row
    place_copy = pltpu.make_async_copy(place_ref, given.at[0], sem.at[0])
    segment_copy = pltpu.make_async_copy(segment_ref, given.at[1], sem.at[1])
    place_copy.start()
    segment_copy.start()
    for c in range(STEPS):
        fetch(c, k_ref, k_held, k_sem).start()
        fetch(c, v_ref, v_held, v_sem).start()
        fetch(c, q_ref, q_held, q_sem).start()

    def step(c, carry):
        fetch(c, k_ref, k_held, k_sem).wait()
        fetch(c, v_ref, v_held, v_sem).wait()
        fetch(c, q_ref, q_held, q_sem).wait()
        for j in range(STEP):
            block = c * STEP + j
            rows = rows_at(block * BLOCK, BLOCK)
            for h in range(HEADS_DEV):
                turned = k_held[rows, head_cols(h)].T
                state = jnp.dot(turned, v_held[rows, head_cols(h)], preferred_element_type=F32)
                own_ref[h * PARTS : (h + 1) * PARTS, rows_at(block * SLICE, SLICE)] = (
                    state.astype(BF16).reshape(PARTS, SLICE, HD)
                )
                scores = jnp.dot(q_held[rows, head_cols(h)], turned, preferred_element_type=F32)
                scores_ref[rows, head_cols(h)] = jnp.where(causal, scores, 0.0).astype(BF16)
        return carry

    lax.fori_loop(0, STEPS, step, 0)
    place_copy.wait()
    segment_copy.wait()
    place = given[0]
    owner = lax.shift_right_logical(place * 2731, 16)
    plan[...] = jnp.zeros_like(plan)
    plan[0:1, 0:BLOCKS_DEV] = owner
    plan[1:2, 0:BLOCKS_DEV] = place - owner * BLOCKS_DEV
    plan[2:3, SEGMENT_AT : SEGMENT_AT + BLOCKS_DEV] = given[1]
    own_ref[:, SENT : SENT + PLAN] = jnp.broadcast_to(
        plan[...].astype(F32).astype(BF16)[None], (SEQ, PLAN, HD)
    )


def states(queries, keys, values, placement, segments):
    held = pltpu.VMEM((TOKENS_DEV, FEATURES), BF16)
    return pl.pallas_call(
        states_kernel,
        in_specs=[HBM] * 5,
        out_specs=[VMEM, VMEM],
        out_shape=[pltpu.VMEM((SEQ, SENT + PLAN, HD), BF16), held],
        scratch_shapes=[
            held,
            held,
            held,
            pltpu.VMEM((2, 1, BLOCKS_DEV), I32),
            pltpu.VMEM((PLAN, HD), I32),
            pltpu.SemaphoreType.DMA((STEPS,)),
            pltpu.SemaphoreType.DMA((STEPS,)),
            pltpu.SemaphoreType.DMA((STEPS,)),
            pltpu.SemaphoreType.DMA((2,)),
        ],
        compiler_params=params(22),
        name="block_states",
    )(
        in_hbm(queries),
        in_hbm(keys),
        in_hbm(values),
        in_hbm(placement.reshape(1, BLOCKS_DEV)),
        in_hbm(segments.reshape(1, BLOCKS_DEV)),
    )


def block_order(got_ref):
    plan = got_ref[:, SENT : SENT + PLAN].astype(F32)
    spot_row = lax.broadcasted_iota(I32, (SEQ, HD), 0).astype(F32)
    lane = lax.broadcasted_iota(I32, (SEQ, HD), 1)
    slot = lane.astype(F32)
    real = lane < BLOCKS_DEV
    owner_row = jnp.where(real, spot_row, -1.0)
    picks, spots = [], []
    for d in range(SEQ):
        picks.append(jnp.where(plan[d, 0:1] == owner_row, 1.0, 0.0).astype(BF16))
        here = plan[d, 1:2] == spot_row
        spots.append(
            jnp.concatenate(
                [jnp.where(here, float(d), 0.0), jnp.where(here, slot, 0.0)], axis=0
            ).astype(BF16)
        )
    found = lax.dot_general(
        jnp.concatenate(picks, axis=1),
        jnp.concatenate(spots, axis=1),
        (((1,), (1,)), ((), ())),
        preferred_element_type=F32,
    ).astype(I32)
    loader, slot = found[:, :SEQ], found[:, SEQ:]
    got_at = loader * (SENT + PLAN) + slot * SLICE
    out_at = loader * SENT + slot * SLICE
    rows = jnp.concatenate([got_at, out_at, jnp.zeros((SEQ, HD - 2 * SEQ), I32)], axis=1)
    return jnp.where(lane < SEGMENT_AT, rows, plan[:, 2, :].astype(I32))


def prefix_kernel(got_ref, out_ref, order, table, order_sem):
    order[...] = block_order(got_ref)
    order_copy = pltpu.make_async_copy(order, table, order_sem)
    order_copy.start()
    order_copy.wait()
    got_rows = got_ref.reshape(SEQ * (SENT + PLAN), HD)
    out_rows = out_ref.reshape(SEQ * SENT, HD)

    def owner_step(o, carry):
        for first in range(0, BLOCKS_DEV, GROUP):
            group = range(first, first + GROUP)

            def run(total, last, check):
                for start in range(group[0], group[-1] + 1, LOADED):
                    part = range(start, start + LOADED)
                    loaded = [
                        got_rows[pl.ds(pl.multiple_of(table[o, w], PLAN), SLICE), :] for w in part
                    ]
                    before = []
                    for w, state in zip(part, loaded):
                        if check:
                            segment = table[o, SEGMENT_AT + w]
                            total = jnp.where(segment == last, total, 0.0)
                            last = segment
                        before.append(total.astype(BF16))
                        total = total + state.astype(F32)
                    for w, value in zip(part, before):
                        out_rows[rows_at(table[o, OUT_AT + w], SLICE), :] = value
                return total, last

            total, last = carry
            carry = lax.cond(
                table[o, SEGMENT_AT + group[-1]] == last,
                lambda total, last: run(total, last, False),
                lambda total, last: run(total, last, True),
                total,
                last,
            )
        return carry

    lax.fori_loop(0, SEQ, owner_step, (jnp.zeros((SLICE, HD), F32), I32(-1)))


def prefix(got):
    return pl.pallas_call(
        prefix_kernel,
        in_specs=[VMEM],
        out_specs=VMEM,
        out_shape=pltpu.VMEM((SEQ, SENT, HD), BF16),
        scratch_shapes=[
            pltpu.VMEM((SEQ, HD), I32),
            pltpu.SMEM((SEQ, HD), I32),
            pltpu.SemaphoreType.DMA,
        ],
        compiler_params=params(8),
        name="prefix",
    )(in_vmem(got))


def attend_kernel(q_ref, scores_ref, v_ref, carried_ref, out_ref, square_ref):
    def step(c, carry):
        for j in range(ATTEND_STEP):
            block = c * ATTEND_STEP + j
            rows = rows_at(block * BLOCK, BLOCK)
            squares = jnp.zeros((BLOCK, HD), F32)
            for h in range(HEADS_DEV):
                carried = carried_ref[
                    h * PARTS : (h + 1) * PARTS, rows_at(block * SLICE, SLICE)
                ].reshape(HD, HD)
                attended = jnp.dot(
                    jnp.concatenate(
                        [scores_ref[rows, head_cols(h)], q_ref[rows, head_cols(h)]], axis=1
                    ),
                    jnp.concatenate([v_ref[rows, head_cols(h)], carried], axis=0),
                    preferred_element_type=F32,
                )
                out_ref[rows, head_cols(h)] = attended
                squares = squares + attended * attended
            square_ref[pl.ds(block, 1), :] = jnp.sum(squares.T, axis=0, keepdims=True)
        return carry

    lax.fori_loop(0, BLOCKS_DEV // ATTEND_STEP, step, 0)


def attend(queries, scores, values, carried):
    return pl.pallas_call(
        attend_kernel,
        in_specs=[VMEM] * 4,
        out_specs=[VMEM, VMEM],
        out_shape=[
            pltpu.VMEM((TOKENS_DEV, FEATURES), F32),
            jax.ShapeDtypeStruct((BLOCKS_DEV, BLOCK), F32),
        ],
        compiler_params=params(8),
        name="attend",
    )(in_vmem(queries), in_vmem(scores), in_vmem(values), in_vmem(carried))


def finish_kernel(width, attended_ref, gain_ref, *refs):
    square_refs, (out_ref, staged, out_sem) = refs[:-3], refs[-3:]
    total = square_refs[0][...]
    for ref in square_refs[1:]:
        total = total + ref[...]
    scaling = lax.rsqrt(total / width + 1e-05)

    def give(c):
        rows = slice(c * STEP * BLOCK, (c + 1) * STEP * BLOCK)
        return pltpu.make_async_copy(staged.at[rows], out_ref.at[rows], out_sem.at[c])

    for c in range(STEPS):
        for block in range(c * STEP, (c + 1) * STEP):
            rows = slice(block * BLOCK, (block + 1) * BLOCK)
            factor = jnp.broadcast_to(scaling[block : block + 1, :], (HD, BLOCK)).T
            for h in range(HEADS_DEV):
                at = (rows, head_cols(h))
                staged[at] = (attended_ref[at] * factor * gain_ref[:, head_cols(h)]).astype(BF16)
        give(c).start()
    for c in range(STEPS):
        give(c).wait()


def finish(attended, gain, squares, width):
    return pl.pallas_call(
        lambda *refs: finish_kernel(width, *refs),
        in_specs=[VMEM] * (2 + len(squares)),
        out_specs=HBM,
        out_shape=jax.ShapeDtypeStruct((TOKENS_DEV, FEATURES), BF16),
        scratch_shapes=[
            pltpu.VMEM((TOKENS_DEV, FEATURES), BF16),
            pltpu.SemaphoreType.DMA((STEPS,)),
        ],
        compiler_params=params(12),
        name="finish_rows",
    )(in_vmem(attended), gain.reshape(1, FEATURES), *squares)


def to_all(value):
    return lax.all_to_all(value, "seq", split_axis=0, concat_axis=0, tiled=True)


def on_device(queries, keys, values, gain, placement, segments):
    head_count = lax.axis_size("head")
    own, scores = states(queries, keys, values, placement, segments)
    attended, square = attend(queries, scores, values, to_all(prefix(to_all(own))))
    squares = [square] + [
        lax.ppermute(square, "head", [(i, (i + s) % head_count) for i in range(head_count)])
        for s in range(1, head_count)
    ]
    return finish(attended, gain, squares, head_count * FEATURES)


def solution(mesh):
    return jax.shard_map(
        on_device,
        mesh=mesh,
        in_specs=(
            P("seq", "head"),
            P("seq", "head"),
            P("seq", "head"),
            P("head"),
            P("seq"),
            P("seq"),
        ),
        out_specs=P("seq", "head"),
        check_vma=False,
    )
```

```python
import jax
import jax.numpy as jnp
from jax import lax
from jax.experimental import pallas as pl
from jax.experimental.pallas import tpu as pltpu
from jax.sharding import PartitionSpec as P

HD = 128
BLOCK = 128
BLOCKS_DEV = 24
HEADS_DEV = 8
SEQ = 32
NBLOCK = SEQ * BLOCKS_DEV
TOKENS_DEV = BLOCKS_DEV * BLOCK
FEATURES = HEADS_DEV * HD
SLICE = FEATURES // SEQ
PARTS = HD // SLICE
SENT = BLOCKS_DEV * SLICE
PLAN = 16
STEP = 3
STEPS = BLOCKS_DEV // STEP
ATTEND_STEP = 24
GROUP = 24
LOADED = 8
OUT_AT = SEQ
SEGMENT_AT = 2 * SEQ
MIB = 1 << 20
F32 = jnp.float32
BF16 = jnp.bfloat16
I32 = jnp.int32
VMEM = pl.BlockSpec(memory_space=pltpu.VMEM)
HBM = pl.BlockSpec(memory_space=pltpu.HBM)


def params(mib):
    return pltpu.CompilerParams(vmem_limit_bytes=mib * MIB)


def head_cols(h):
    return slice(h * HD, (h + 1) * HD)


def rows_at(start, size):
    return pl.ds(pl.multiple_of(start, size), size)


def in_vmem(value):
    return pltpu.with_memory_space_constraint(value, pltpu.VMEM)


def in_hbm(value):
    return pltpu.with_memory_space_constraint(value, pltpu.HBM)


def step_rows(c):
    return rows_at(c * STEP * BLOCK, STEP * BLOCK)


def states_kernel(
    q_ref, k_ref, v_ref, place_ref, segment_ref, own_ref, scores_ref, q_held, k_held, v_held, given,
    plan, q_sem, k_sem, v_sem, sem
):
    def fetch(c, source, target, sem):
        return pltpu.make_async_copy(source.at[step_rows(c)], target.at[step_rows(c)], sem.at[c])

    row = lax.broadcasted_iota(I32, (BLOCK, BLOCK), 0)
    col = lax.broadcasted_iota(I32, (BLOCK, BLOCK), 1)
    causal = col <= row
    place_copy = pltpu.make_async_copy(place_ref, given.at[0], sem.at[0])
    segment_copy = pltpu.make_async_copy(segment_ref, given.at[1], sem.at[1])
    place_copy.start()
    segment_copy.start()
    for c in range(STEPS):
        fetch(c, k_ref, k_held, k_sem).start()
        fetch(c, v_ref, v_held, v_sem).start()
        fetch(c, q_ref, q_held, q_sem).start()

    def step(c, carry):
        fetch(c, k_ref, k_held, k_sem).wait()
        fetch(c, v_ref, v_held, v_sem).wait()
        fetch(c, q_ref, q_held, q_sem).wait()
        for j in range(STEP):
            block = c * STEP + j
            rows = rows_at(block * BLOCK, BLOCK)
            for h in range(HEADS_DEV):
                turned = k_held[rows, head_cols(h)].T
                state = jnp.dot(turned, v_held[rows, head_cols(h)], preferred_element_type=F32)
                own_ref[h * PARTS : (h + 1) * PARTS, rows_at(block * SLICE, SLICE)] = (
                    state.astype(BF16).reshape(PARTS, SLICE, HD)
                )
                scores = jnp.dot(q_held[rows, head_cols(h)], turned, preferred_element_type=F32)
                scores_ref[rows, head_cols(h)] = jnp.where(causal, scores, 0.0).astype(BF16)
        return carry

    lax.fori_loop(0, STEPS - 1, step, 0)
    place_copy.wait()
    segment_copy.wait()
    place = given[0]
    owner = lax.shift_right_logical(place * 2731, 16)
    plan[...] = jnp.zeros_like(plan)
    plan[0:1, 0:BLOCKS_DEV] = owner
    plan[1:2, 0:BLOCKS_DEV] = place - owner * BLOCKS_DEV
    plan[2:3, SEGMENT_AT : SEGMENT_AT + BLOCKS_DEV] = given[1]
    own_ref[:, SENT : SENT + PLAN] = jnp.broadcast_to(
        plan[...].astype(F32).astype(BF16)[None], (SEQ, PLAN, HD)
    )
    lax.fori_loop(STEPS - 1, STEPS, step, 0)


def states(queries, keys, values, placement, segments):
    held = pltpu.VMEM((TOKENS_DEV, FEATURES), BF16)
    return pl.pallas_call(
        states_kernel,
        in_specs=[HBM] * 5,
        out_specs=[VMEM, VMEM],
        out_shape=[pltpu.VMEM((SEQ, SENT + PLAN, HD), BF16), held],
        scratch_shapes=[
            held,
            held,
            held,
            pltpu.VMEM((2, 1, BLOCKS_DEV), I32),
            pltpu.VMEM((PLAN, HD), I32),
            pltpu.SemaphoreType.DMA((STEPS,)),
            pltpu.SemaphoreType.DMA((STEPS,)),
            pltpu.SemaphoreType.DMA((STEPS,)),
            pltpu.SemaphoreType.DMA((2,)),
        ],
        compiler_params=params(22),
        name="block_states",
    )(
        in_hbm(queries),
        in_hbm(keys),
        in_hbm(values),
        in_hbm(placement.reshape(1, BLOCKS_DEV)),
        in_hbm(segments.reshape(1, BLOCKS_DEV)),
    )


def block_order(got_ref):
    plan = got_ref[:, SENT : SENT + PLAN].astype(F32)
    spot_row = lax.broadcasted_iota(I32, (SEQ, HD), 0).astype(F32)
    lane = lax.broadcasted_iota(I32, (SEQ, HD), 1)
    slot = lane.astype(F32)
    real = lane < BLOCKS_DEV
    owner_row = jnp.where(real, spot_row, -1.0)
    picks, spots = [], []
    for d in range(SEQ):
        picks.append(jnp.where(plan[d, 0:1] == owner_row, 1.0, 0.0).astype(BF16))
        here = plan[d, 1:2] == spot_row
        spots.append(
            jnp.concatenate(
                [jnp.where(here, float(d), 0.0), jnp.where(here, slot, 0.0)], axis=0
            ).astype(BF16)
        )
    found = lax.dot_general(
        jnp.concatenate(picks, axis=1),
        jnp.concatenate(spots, axis=1),
        (((1,), (1,)), ((), ())),
        preferred_element_type=F32,
    ).astype(I32)
    loader, slot = found[:, :SEQ], found[:, SEQ:]
    got_at = loader * (SENT + PLAN) + slot * SLICE
    out_at = loader * SENT + slot * SLICE
    rows = jnp.concatenate([got_at, out_at, jnp.zeros((SEQ, HD - 2 * SEQ), I32)], axis=1)
    return jnp.where(lane < SEGMENT_AT, rows, plan[:, 2, :].astype(I32))


def prefix_kernel(got_ref, out_ref, order, table, order_sem):
    order[...] = block_order(got_ref)
    order_copy = pltpu.make_async_copy(order, table, order_sem)
    order_copy.start()
    order_copy.wait()
    got_rows = got_ref.reshape(SEQ * (SENT + PLAN), HD)
    out_rows = out_ref.reshape(SEQ * SENT, HD)

    def owner_step(o, carry):
        for first in range(0, BLOCKS_DEV, GROUP):
            group = range(first, first + GROUP)

            def run(total, last, check):
                for start in range(group[0], group[-1] + 1, LOADED):
                    part = range(start, start + LOADED)
                    loaded = [
                        got_rows[pl.ds(pl.multiple_of(table[o, w], PLAN), SLICE), :] for w in part
                    ]
                    before = []
                    for w, state in zip(part, loaded):
                        if check:
                            segment = table[o, SEGMENT_AT + w]
                            total = jnp.where(segment == last, total, 0.0)
                            last = segment
                        before.append(total.astype(BF16))
                        total = total + state.astype(F32)
                    for w, value in zip(part, before):
                        out_rows[rows_at(table[o, OUT_AT + w], SLICE), :] = value
                return total, last

            total, last = carry
            carry = lax.cond(
                table[o, SEGMENT_AT + group[-1]] == last,
                lambda total, last: run(total, last, False),
                lambda total, last: run(total, last, True),
                total,
                last,
            )
        return carry

    lax.fori_loop(0, SEQ, owner_step, (jnp.zeros((SLICE, HD), F32), I32(-1)))


def prefix(got):
    return pl.pallas_call(
        prefix_kernel,
        in_specs=[VMEM],
        out_specs=VMEM,
        out_shape=pltpu.VMEM((SEQ, SENT, HD), BF16),
        scratch_shapes=[
            pltpu.VMEM((SEQ, HD), I32),
            pltpu.SMEM((SEQ, HD), I32),
            pltpu.SemaphoreType.DMA,
        ],
        compiler_params=params(8),
        name="prefix",
    )(in_vmem(got))


def attend_kernel(q_ref, scores_ref, v_ref, carried_ref, out_ref, square_ref):
    def step(c, carry):
        for j in range(ATTEND_STEP):
            block = c * ATTEND_STEP + j
            rows = rows_at(block * BLOCK, BLOCK)
            squares = jnp.zeros((BLOCK, HD), F32)
            for h in range(HEADS_DEV):
                carried = carried_ref[
                    h * PARTS : (h + 1) * PARTS, rows_at(block * SLICE, SLICE)
                ].reshape(HD, HD)
                attended = jnp.dot(
                    jnp.concatenate(
                        [scores_ref[rows, head_cols(h)], q_ref[rows, head_cols(h)]], axis=1
                    ),
                    jnp.concatenate([v_ref[rows, head_cols(h)], carried], axis=0),
                    preferred_element_type=F32,
                )
                out_ref[rows, head_cols(h)] = attended
                squares = squares + attended * attended
            square_ref[pl.ds(block, 1), :] = jnp.sum(squares.T, axis=0, keepdims=True)
        return carry

    lax.fori_loop(0, BLOCKS_DEV // ATTEND_STEP, step, 0)


def attend(queries, scores, values, carried):
    return pl.pallas_call(
        attend_kernel,
        in_specs=[VMEM] * 4,
        out_specs=[VMEM, VMEM],
        out_shape=[
            pltpu.VMEM((TOKENS_DEV, FEATURES), F32),
            jax.ShapeDtypeStruct((BLOCKS_DEV, BLOCK), F32),
        ],
        compiler_params=params(8),
        name="attend",
    )(in_vmem(queries), in_vmem(scores), in_vmem(values), in_vmem(carried))


def finish_kernel(width, attended_ref, gain_ref, *refs):
    square_refs, (out_ref, staged, out_sem) = refs[:-3], refs[-3:]
    total = square_refs[0][...]
    for ref in square_refs[1:]:
        total = total + ref[...]
    scaling = lax.rsqrt(total / width + 1e-05)

    def give(c):
        rows = slice(c * STEP * BLOCK, (c + 1) * STEP * BLOCK)
        return pltpu.make_async_copy(staged.at[rows], out_ref.at[rows], out_sem.at[c])

    for c in range(STEPS):
        for block in range(c * STEP, (c + 1) * STEP):
            rows = slice(block * BLOCK, (block + 1) * BLOCK)
            factor = jnp.broadcast_to(scaling[block : block + 1, :], (HD, BLOCK)).T
            for h in range(HEADS_DEV):
                at = (rows, head_cols(h))
                staged[at] = (attended_ref[at] * factor * gain_ref[:, head_cols(h)]).astype(BF16)
        give(c).start()
    for c in range(STEPS):
        give(c).wait()


def finish(attended, gain, squares, width):
    return pl.pallas_call(
        lambda *refs: finish_kernel(width, *refs),
        in_specs=[VMEM] * (2 + len(squares)),
        out_specs=HBM,
        out_shape=jax.ShapeDtypeStruct((TOKENS_DEV, FEATURES), BF16),
        scratch_shapes=[
            pltpu.VMEM((TOKENS_DEV, FEATURES), BF16),
            pltpu.SemaphoreType.DMA((STEPS,)),
        ],
        compiler_params=params(12),
        name="finish_rows",
    )(in_vmem(attended), gain.reshape(1, FEATURES), *squares)


def to_all(value):
    return lax.all_to_all(value, "seq", split_axis=0, concat_axis=0, tiled=True)


def on_device(queries, keys, values, gain, placement, segments):
    head_count = lax.axis_size("head")
    own, scores = states(queries, keys, values, placement, segments)
    attended, square = attend(queries, scores, values, to_all(prefix(to_all(own))))
    squares = [square] + [
        lax.ppermute(square, "head", [(i, (i + s) % head_count) for i in range(head_count)])
        for s in range(1, head_count)
    ]
    return finish(attended, gain, squares, head_count * FEATURES)


def solution(mesh):
    return jax.shard_map(
        on_device,
        mesh=mesh,
        in_specs=(
            P("seq", "head"),
            P("seq", "head"),
            P("seq", "head"),
            P("head"),
            P("seq"),
            P("seq"),
        ),
        out_specs=P("seq", "head"),
        check_vma=False,
    )
```
